32 devices in a mesh: row: 4 (over y, x), col: 8 (over z, core).
Axes of the slice: x: 2, y: 2, z: 4, core: 2. Of those that a mesh axis runs over, the one named last changes fastest.
Arguments:
- trailing: bfloat16 [4096, 8192], P('row', 'col'), may hold values from -6 to 6
- raw_l: bfloat16 [4, 16, 1024, 1024], P('row', None, 'col'), may hold values from -1.1953125 to 1.1953125
- raw_u: bfloat16 [16, 8, 1024, 1024], P(None, 'col', 'row'), may hold values from -1.1953125 to 1.1953125
- sketch: bfloat16 [4, 8, 1024, 192], P('row', 'col'), may hold values from -0.1875 to 0.1875
- helper_l: int32 [4, 16], P('row'), may hold values from 0 to 7, as said below
- helper_u: int32 [16, 8], P(None, 'col'), may hold values from 0 to 3, as said below
- ranks_l: int32 [4, 16], P('row'), may hold values from 64 to 192, as said below
- ranks_u: int32 [16, 8], P(None, 'col'), may hold values from 64 to 192, as said below
Outputs:
- updated: float32 [4096, 8192], P('row', 'col')
The draws below stay inside these ranges and needn't reach their ends.
Inputs may be any that keep to these rules, and one draw needn't show every extreme that they name: `helper_l`: in every grid row no value occurs more than 4 times, and some value occurs exactly 4 times. `helper_u`: in every grid column no value occurs more than 8 times, and some value occurs exactly 8 times. `ranks_l`: some tile has rank 64 and some tile rank 192. `ranks_u`: some tile has rank 64 and some tile rank 192.
All inputs are finite; a program needn't handle non-finite values.
Results may differ from the reference program's by a relative error of at most 0.0068.
Values may be sent and summed in bfloat16 or wider, within the bound.
No kernel may reach another device: no remote copies, remote signals or barrier semaphores. Data moves between devices by JAX's collectives and lax.ppermute only.
A program may use at most 192 MiB of HBM per device.

```python
import jax
import jax.numpy as jnp
from jax import lax

B = 1024
RMAX = 192
RLO = 64
KD = 16
CAP_L = 4
CAP_U = 8
N_ROW = 4
N_COL = 8


def spread_helpers(key, groups, count, owners, capacity):

    def one_group(group):
        group_key = jax.random.fold_in(key, group)
        order = jax.random.permutation(group_key, owners * capacity).astype(jnp.int32)
        chosen = order[0] // capacity
        for place in range(capacity):
            partner = chosen * capacity + place
            where_at = jnp.argmax(order == partner)
            moved = order[place]
            order = order.at[where_at].set(moved).at[place].set(partner)
        return order[:count] // capacity
    return jax.vmap(one_group)(jnp.arange(groups, dtype=jnp.int32))


def pick_ranks(key, shape):
    values = jax.random.randint(key, shape, RLO, RMAX + 1, dtype=jnp.int32).reshape(-1)
    total = values.shape[0]
    first = jax.random.randint(jax.random.fold_in(key, 1), (), 0, total, dtype=jnp.int32)
    offset = jax.random.randint(jax.random.fold_in(key, 2), (), 0, total - 1, dtype=jnp.int32)
    second = (first + 1 + offset) % total
    values = values.at[first].set(RMAX).at[second].set(RLO)
    return values.reshape(shape)


def draw_helper_l(key, part):
    return spread_helpers(jax.random.fold_in(key, 11), N_ROW, KD, N_COL, CAP_L)


def draw_helper_u(key, part):
    return spread_helpers(jax.random.fold_in(key, 13), N_COL, KD, N_ROW, CAP_U).T


def draw_ranks_l(key, part):
    return pick_ranks(jax.random.fold_in(key, 17), (N_ROW, KD))


def draw_ranks_u(key, part):
    return pick_ranks(jax.random.fold_in(key, 19), (KD, N_COL))


def shard_levels(rng, extent, split, least, largest):
    def one(position, shards_of):
        heights = jax.random.uniform(jax.random.fold_in(jax.random.fold_in(rng, 6), position), (shards_of,), jnp.float32, least / len(split), largest / len(split))
        return jnp.repeat(jnp.exp(heights), extent[position] // shards_of).reshape((-1,) + (1,) * (len(extent) - position - 1))

    factor_of = one(*split[0])
    for cut in split[1:]:
        factor_of = factor_of * one(*cut)
    return factor_of


def gaussian(key, dims, width, limit, cuts=(), kind=jnp.bfloat16):
    values = jax.random.normal(key, dims, jnp.float32) * width
    if len(cuts) > 0:
        values = shard_levels(key, dims, cuts, -0.22, 0.18) * values
    return jnp.clip(values, min=-limit, max=limit).astype(kind)


def setup_inputs(seed: int = 0) -> dict:
    key_list = jax.random.split(jax.random.key(seed), 9)
    return {
        "trailing": gaussian(key_list[0], (N_ROW * B, N_COL * B), 1.0, 6.0, ((0, 4), (1, 8))),
        "raw_l": gaussian(key_list[1], (N_ROW, KD, B, B), 0.2, 1.1953125, ((0, 4), (2, 8))),
        "raw_u": gaussian(key_list[2], (KD, N_COL, B, B), 0.2, 1.1953125, ((1, 8), (2, 4))),
        "sketch": gaussian(key_list[3], (N_ROW, N_COL, B, RMAX), B ** -0.5, 0.1875, ((0, 4), (1, 8))),
        "helper_l": draw_helper_l(jax.random.fold_in(key_list[8], 71), 0),
        "helper_u": draw_helper_u(jax.random.fold_in(key_list[8], 71), 0),
        "ranks_l": draw_ranks_l(jax.random.fold_in(key_list[8], 71), 0),
        "ranks_u": draw_ranks_u(jax.random.fold_in(key_list[8], 71), 0),
    }


def compress_tile(panel_tile, tile_rank, sketch_cols):
    keep_cols = jnp.arange(sketch_cols.shape[1]) < tile_rank
    masked = jnp.where(keep_cols[None, :], sketch_cols, jnp.zeros_like(sketch_cols))
    sketched = jnp.dot(panel_tile.astype(jnp.float32), masked.astype(jnp.float32), preferred_element_type=jnp.float32)
    padding = jnp.where(keep_cols, 1.0, 1.0) - jnp.where(keep_cols, 1.0, 0.0)
    gram = jnp.dot(sketched.T, sketched, precision=lax.Precision.HIGHEST) + jnp.diag(padding.astype(jnp.float32))
    lower_factor = jnp.linalg.cholesky(gram)
    basis = jax.scipy.linalg.solve_triangular(lower_factor, sketched.T, lower=True).T.astype(jnp.bfloat16)
    coeffs = lax.dot_general(panel_tile.astype(jnp.float32), basis.astype(jnp.float32), (((0,), (0,)), ((), ())), preferred_element_type=jnp.float32).astype(jnp.bfloat16)
    return jnp.concatenate([basis, coeffs], axis=1)

def reference(trailing, raw_l, raw_u, sketch, helper_l, helper_u, ranks_l, ranks_u):
    width_r = sketch.shape[3]
    grid_rows = jnp.repeat(jnp.arange(N_ROW, dtype=jnp.int32), KD)
    grid_cols = jnp.tile(jnp.arange(N_COL, dtype=jnp.int32), KD)

    def make_row(item):
        panel_tile, tile_rank, grid_row, helper = item
        return compress_tile(panel_tile, tile_rank, sketch[grid_row, helper])

    def make_col(item):
        panel_tile, tile_rank, grid_col, helper = item
        return compress_tile(panel_tile, tile_rank, sketch[helper, grid_col])
    made_row = lax.map(make_row, (raw_l.reshape(N_ROW * KD, B, B), ranks_l.reshape(-1), grid_rows, helper_l.reshape(-1)))
    made_row = made_row.reshape(N_ROW, KD, B, 2 * width_r)
    made_col = lax.map(make_col, (raw_u.reshape(KD * N_COL, B, B), ranks_u.reshape(-1), grid_cols, helper_u.reshape(-1)))
    made_col = made_col.reshape(KD, N_COL, B, 2 * width_r)

    def update_tile(pair):
        grid_row = (pair // N_COL).astype(jnp.int32)
        grid_col = (pair % N_COL).astype(jnp.int32)
        full_row = made_row[grid_row].astype(jnp.float32)
        full_col = made_col[:, grid_col].astype(jnp.float32)
        middle = jnp.einsum('kbr,kbs->krs', full_row[:, :, width_r:], full_col[:, :, :width_r])
        middle = lax.optimization_barrier(middle.astype(jnp.bfloat16)).astype(jnp.float32)
        left = jnp.einsum('kbr,krs->kbs', full_row[:, :, :width_r], middle)
        left = lax.optimization_barrier(left.astype(jnp.bfloat16)).astype(jnp.float32)
        update = jnp.einsum('kbs,kcs->bc', left, full_col[:, :, width_r:])
        start = lax.dynamic_slice(trailing, ((grid_row * B).astype(jnp.int32), (grid_col * B).astype(jnp.int32)), (B, B))
        return start.astype(jnp.float32) - update
    tiles = lax.map(update_tile, jnp.arange(N_ROW * N_COL, dtype=jnp.int32))
    return tiles.reshape(N_ROW, N_COL, B, B).transpose(0, 2, 1, 3).reshape(N_ROW * B, N_COL * B)
```

```python
import functools

import jax
import jax.numpy as jnp
from jax import lax
from jax.experimental import pallas as pl
from jax.experimental.pallas import tpu as pltpu
from jax.sharding import PartitionSpec as P

NB = 32
HIGH = lax.Precision.HIGHEST
NN = (((1,), (0,)), ((), ()))
NT = (((1,), (1,)), ((), ()))
TN = (((0,), (0,)), ((), ()))


def mm(a, b, dims, precision=None):
    return lax.dot_general(a, b, dims, precision=precision, preferred_element_type=jnp.float32)


def invert_diagonal(blocks):
    nb = blocks[0].shape[0]
    row = lax.broadcasted_iota(jnp.int32, (nb, 2 * nb), 0)
    lane = lax.broadcasted_iota(jnp.int32, (nb, 2 * nb), 1)
    eye = (lane == row + nb).astype(jnp.float32)
    work = [jnp.concatenate([b, eye[:, nb:]], axis=1) for b in blocks]
    for j in range(nb - 1):
        for n, a in enumerate(work):
            pivot_row = a[j : j + 1, :]
            scaled = pivot_row / a[j : j + 1, j : j + 1]
            work[n] = a - jnp.where(row > j, a[:, j : j + 1], 0.0) * scaled
    out = []
    for a in work:
        d = jnp.sum(jnp.where(lane == row, a, 0.0), axis=1, keepdims=True)
        r = lax.rsqrt(d)
        r = r * (1.5 - 0.5 * d * r * r)
        out.append(a[:, nb:] * r)
    return out


def invert_cholesky(z_ref, n, width):
    for j in range(width // NB):
        lo, hi = j * NB, (j + 1) * NB
        inverses = invert_diagonal([z_ref[t, lo:hi, lo:hi] for t in range(n)])
        for t in range(n):
            panel = mm(inverses[t], z_ref[t, lo:hi, :], NN, HIGH)
            z_ref[t, lo:hi, :] = panel
            if hi < width:
                z_ref[t, hi:, :] = z_ref[t, hi:, :] - mm(panel[:, hi:width], panel, TN, HIGH)


def factor_kernel(n_l, n_u, n_col, n_row, *refs):
    place, help_l, rank_l, help_u, rank_u = refs[:5]
    raw_l, raw_u, sk_col, sk_row = refs[5:9]
    got_l = refs[9 : 9 + n_col - 1]
    got_u = refs[9 + n_col - 1 : 9 + n_col + n_row - 2]
    rest = refs[9 + n_col + n_row - 2 :]
    q_out = rest[0]
    w_out = rest[1]
    tile, omega, sketched, z, sem, sem_s = rest[2:]
    my_row, my_col = place[0], place[1]
    width = omega.shape[1]
    order = tile.shape[1]
    n = n_l + n_u
    slab_l, slab_u = order // n_col, order // n_row

    def rows(start, count):
        return pl.ds(pl.multiple_of(start * count, count), count)

    copies = []
    for t in range(n):
        mine = []
        if t < n_l:
            k = t * n_col + my_col
            mine.append(pltpu.make_async_copy(sk_col.at[help_l[k]], omega.at[t], sem_s.at[t]))
            for d in range(n_col):
                j = lax.rem(my_col - d + n_col, n_col)
                src = raw_l.at[k] if d == 0 else got_l[d - 1].at[t]
                mine.append(pltpu.make_async_copy(src, tile.at[t, rows(j, slab_l)], sem.at[t, d]))
        else:
            i = t - n_l
            k = i * n_row + my_row
            mine.append(pltpu.make_async_copy(sk_row.at[help_u[k]], omega.at[t], sem_s.at[t]))
            for d in range(n_row):
                j = jnp.bitwise_xor(my_row, d)
                src = raw_u.at[k] if d == 0 else got_u[d - 1].at[i]
                mine.append(pltpu.make_async_copy(src, tile.at[t, rows(j, slab_u)], sem.at[t, d]))
        for c in mine:
            c.start()
        copies.append(mine)

    row = lax.broadcasted_iota(jnp.int32, (width, width), 0)
    lane = lax.broadcasted_iota(jnp.int32, (width, width), 1)
    eye = (row == lane).astype(jnp.float32)
    sub = lax.broadcasted_iota(jnp.int32, (width, order), 0)
    for t in range(n):
        for c in copies[t]:
            c.wait()
        q = rank_l[t * n_col + my_col] if t < n_l else rank_u[(t - n_l) * n_row + my_row]
        masked = jnp.where(sub < q, omega[t].astype(jnp.float32), 0.0).astype(jnp.bfloat16)
        sketched[t] = mm(masked, tile[t], NT)
        gram = mm(sketched[t], sketched[t], NT, HIGH) + jnp.where(row >= q, eye, 0.0)
        z[t] = jnp.concatenate([gram, eye], axis=1)
    invert_cholesky(z, n, width)
    for t in range(n):
        basis = mm(z[t, :, width:], sketched[t], NN, HIGH).astype(jnp.bfloat16)
        q_out[t] = basis
        w_out[t] = mm(basis, tile[t], NN).astype(jnp.bfloat16)


def factor(place, help_l, rank_l, help_u, rank_u, raw_l, raw_u, sk_col, sk_row, got_l, got_u):
    n_col, n_row = len(got_l) + 1, len(got_u) + 1
    n_l, n_u = raw_l.shape[0] // n_col, raw_u.shape[0] // n_row
    n = n_l + n_u
    width, order = sk_col.shape[1:]
    smem = pl.BlockSpec(memory_space=pltpu.SMEM)
    hbm = pl.BlockSpec(memory_space=pl.ANY)
    vmem = pl.BlockSpec(memory_space=pltpu.VMEM)
    made = jax.ShapeDtypeStruct((n, width, order), jnp.bfloat16)
    return pl.pallas_call(
        functools.partial(factor_kernel, n_l, n_u, n_col, n_row),
        out_shape=(made, made),
        in_specs=[smem] * 5 + [hbm] * (4 + n_col + n_row - 2),
        out_specs=(vmem, vmem),
        scratch_shapes=[
            pltpu.VMEM((n, order, order), jnp.bfloat16),
            pltpu.VMEM((n, width, order), jnp.bfloat16),
            pltpu.VMEM((n, width, order), jnp.float32),
            pltpu.VMEM((n, width, 2 * width), jnp.float32),
            pltpu.SemaphoreType.DMA((n, max(n_col, n_row))),
            pltpu.SemaphoreType.DMA((n,)),
        ],
        compiler_params=pltpu.CompilerParams(vmem_limit_bytes=56 * 2**20),
        name="factor_tiles",
    )(place, help_l, rank_l, help_u, rank_u, raw_l, raw_u, sk_col, sk_row, *got_l, *got_u)


def update_kernel(n_l, n_u, n_col, n_row, group, *refs):
    place, trailing = refs[:2]
    at = 2
    lq = refs[at : at + n_col]
    at += n_col
    lw = refs[at : at + n_col]
    at += n_col
    uq = refs[at : at + 2 * n_row]
    at += 2 * n_row
    uw = refs[at : at + 2 * n_row]
    at += 2 * n_row
    out, ql, wl, qu, wu, left, sem, sem_t, tr = refs[at:]
    my_row, my_col = place[0], place[1]
    width = ql.shape[1]
    chips = n_col // 2
    chip, core = my_col // 2, lax.rem(my_col, 2)
    half = n_u // 2
    depth = n_l * n_col
    load = pltpu.make_async_copy(trailing, tr, sem_t)
    load.start()

    def start_l(i):
        for s in range(chips):
            for x in range(2):
                f = 2 * lax.rem(chip - s + chips, chips) + jnp.bitwise_xor(core, x)
                k = i * n_col + f
                pltpu.make_async_copy(lw[2 * s + x].at[i], wl.at[k], sem.at[1, k]).start()
                pltpu.make_async_copy(lq[2 * s + x].at[i], ql.at[k], sem.at[0, k]).start()

    def start_u(j):
        for o in range(n_row):
            k = j * n_row + jnp.bitwise_xor(my_row, o)
            src = 2 * o + j // half
            pltpu.make_async_copy(uq[src].at[j % half], qu.at[k], sem.at[2, k]).start()
            pltpu.make_async_copy(uw[src].at[j % half], wu.at[k], sem.at[3, k]).start()

    per = n_u // n_l
    for i in range(n_l):
        for j in range(i * per, (i + 1) * per):
            start_u(j)
        start_l(i)
    load.wait()
    out[...] = tr[...].astype(jnp.float32)

    def one_group(g, carry):
        for e in range(group):
            k = g * group + e
            for a, buf in enumerate((ql, wl, qu, wu)):
                pltpu.make_async_copy(buf.at[k], buf.at[k], sem.at[a, k]).wait()
            mid = mm(qu[k], wl[k], NT).astype(jnp.bfloat16)
            left[e * width : (e + 1) * width, :] = mm(mid, ql[k], NN).astype(jnp.bfloat16)
        coeff = wu[pl.ds(g * group, group)].reshape(group * width, wu.shape[2])
        out[...] = out[...] - mm(left[...], coeff, TN)
        return carry

    lax.fori_loop(0, depth // group, one_group, 0)


def update(place, trailing, lq, lw, uq, uw, n_l, n_u):
    n_col, n_row = len(lq), len(uq) // 2
    depth = n_l * n_col
    width, order = lq[0].shape[1:]
    group = 4
    smem = pl.BlockSpec(memory_space=pltpu.SMEM)
    hbm = pl.BlockSpec(memory_space=pl.ANY)
    vmem = pl.BlockSpec(memory_space=pltpu.VMEM)
    held = pltpu.VMEM((depth, width, order), jnp.bfloat16)
    return pl.pallas_call(
        functools.partial(update_kernel, n_l, n_u, n_col, n_row, group),
        out_shape=jax.ShapeDtypeStruct(trailing.shape, jnp.float32),
        in_specs=[smem] + [hbm] * (1 + 2 * n_col + 4 * n_row),
        out_specs=vmem,
        scratch_shapes=[held, held, held, held]
        + [
            pltpu.VMEM((group * width, order), jnp.bfloat16),
            pltpu.SemaphoreType.DMA((4, depth)),
            pltpu.SemaphoreType.DMA,
            pltpu.VMEM(trailing.shape, trailing.dtype),
        ],
        compiler_params=pltpu.CompilerParams(vmem_limit_bytes=56 * 2**20),
        name="update_tile",
    )(place, trailing, *lq, *lw, *uq, *uw)


def shift(x, axis, size, move):
    return lax.ppermute(x, axis, [(i, move(i)) for i in range(size)])


def exchange_l(raw, n_col):
    me = lax.axis_index("col")
    x = raw.reshape((-1, n_col) + raw.shape[1:])
    return [
        shift(
            lax.dynamic_index_in_dim(x, lax.rem(me + d, n_col), 1, False),
            "col",
            n_col,
            lambda i: (i + d) % n_col,
        )
        for d in range(1, n_col)
    ]


def exchange_u(raw, n_row):
    me = lax.axis_index("row")
    x = raw.reshape((-1, n_row) + raw.shape[1:])
    return [
        shift(
            lax.dynamic_index_in_dim(x, jnp.bitwise_xor(me, d), 1, False),
            "row",
            n_row,
            lambda i: i ^ d,
        )
        for d in range(1, n_row)
    ]


def gather_col(pieces, n_col):
    chips = n_col // 2
    out = [[] for _ in pieces]
    now = list(pieces)
    for s in range(chips):
        later = [shift(p, "col", n_col, lambda i: (i + 2) % n_col) for p in now] if s + 1 < chips else []
        for o, p in zip(out, now):
            o += [p, shift(p, "col", n_col, lambda i: i ^ 1)]
        now = later
    return out


def gather_row(pieces, n_row):
    bits = [1 << b for b in range(n_row.bit_length() - 1)]
    out = []
    for number, piece in enumerate(pieces):
        turn = number % len(bits)
        held = {0: piece}
        for b in bits[turn:] + bits[:turn]:
            held.update({o ^ b: shift(p, "row", n_row, lambda i: i ^ b) for o, p in held.items()})
        out.append([held[o] for o in range(n_row)])
    return out


def local(trailing, raw_l, raw_u, sketch, helper_l, helper_u, ranks_l, ranks_u):
    n_col, n_row = lax.axis_size("col"), lax.axis_size("row")
    place = jnp.stack([lax.axis_index("row"), lax.axis_index("col")]).astype(jnp.int32)
    mine_l, mine_u = raw_l[0], raw_u[:, 0]
    n_l, n_u = mine_l.shape[0] // n_col, mine_u.shape[0] // n_row
    own = jnp.swapaxes(sketch[0, 0], 0, 1)[None]
    sk_col = lax.all_gather(own, "col", axis=0, tiled=True)
    sk_row = lax.all_gather(own, "row", axis=0, tiled=True)
    got_l = exchange_l(mine_l, n_col)
    got_u = exchange_u(mine_u, n_row)
    q, w = factor(
        place, helper_l[0], ranks_l[0], helper_u[:, 0], ranks_u[:, 0],
        mine_l, mine_u, sk_col, sk_row, got_l, got_u,
    )
    half = n_l + n_u // 2
    lq, lw = gather_col([q[:n_l], w[:n_l]], n_col)
    parts = gather_row([q[n_l:half], q[half:], w[n_l:half], w[half:]], n_row)
    uq = [p for pair in zip(parts[0], parts[1]) for p in pair]
    uw = [p for pair in zip(parts[2], parts[3]) for p in pair]
    return update(place, trailing, lq, lw, uq, uw, n_l, n_u)


def solution(mesh):
    placed = (
        P("row", "col"),
        P("row", None, "col", None),
        P(None, "col", "row", None),
        P("row", "col", None, None),
        P("row", None),
        P(None, "col"),
        P("row", None),
        P(None, "col"),
    )
    return jax.shard_map(
        local, mesh=mesh, in_specs=placed, out_specs=P("row", "col"), check_vma=False
    )
```

```python
import functools

import jax
import jax.numpy as jnp
from jax import lax
from jax.experimental import pallas as pl
from jax.experimental.pallas import tpu as pltpu
from jax.sharding import PartitionSpec as P

NB = 32
HIGH = lax.Precision.HIGHEST
NN = (((1,), (0,)), ((), ()))
NT = (((1,), (1,)), ((), ()))
TN = (((0,), (0,)), ((), ()))


def mm(a, b, dims, precision=None):
    return lax.dot_general(a, b, dims, precision=precision, preferred_element_type=jnp.float32)


def invert_diagonal(blocks):
    nb = blocks[0].shape[0]
    row = lax.broadcasted_iota(jnp.int32, (nb, 2 * nb), 0)
    lane = lax.broadcasted_iota(jnp.int32, (nb, 2 * nb), 1)
    eye = (lane == row + nb).astype(jnp.float32)
    work = [jnp.concatenate([b, eye[:, nb:]], axis=1) for b in blocks]
    for j in range(nb - 1):
        for n, a in enumerate(work):
            pivot_row = a[j : j + 1, :]
            scaled = pivot_row / a[j : j + 1, j : j + 1]
            work[n] = a - jnp.where(row > j, a[:, j : j + 1], 0.0) * scaled
    out = []
    for a in work:
        d = jnp.sum(jnp.where(lane == row, a, 0.0), axis=1, keepdims=True)
        r = lax.rsqrt(d)
        r = r * (1.5 - 0.5 * d * r * r)
        out.append(a[:, nb:] * r)
    return out


def invert_cholesky(z_ref, n, width):
    for j in range(width // NB):
        lo, hi = j * NB, (j + 1) * NB
        inverses = invert_diagonal([z_ref[t, lo:hi, lo:hi] for t in range(n)])
        for t in range(n):
            panel = mm(inverses[t], z_ref[t, lo:hi, :], NN, HIGH)
            z_ref[t, lo:hi, :] = panel
            if hi < width:
                z_ref[t, hi:, :] = z_ref[t, hi:, :] - mm(panel[:, hi:width], panel, TN, HIGH)


def factor_kernel(n_col, n_row, chunk, *refs):
    place, help_l, rank_l, help_u, rank_u = refs[:5]
    tile_l, raw_u, sk_col = refs[5:8]
    sk_row = refs[8 : 8 + n_row]
    got_u = refs[8 + n_row : 7 + 2 * n_row]
    q_l, q_u, omega, tile, sketched, z, sem, sem_s = refs[7 + 2 * n_row :]
    my_row, my_col = place[0], place[1]
    n, width, order = sketched.shape
    slab = order // n_row

    copies = []
    for t in range(n):
        if t == 0:
            k = chunk * n_col + my_col
            mine = [
                pltpu.make_async_copy(sk_col.at[help_l[k]], omega.at[t], sem_s.at[t]),
                pltpu.make_async_copy(tile_l, tile.at[t], sem.at[t, 0]),
            ]
        else:
            k = chunk * n_col + (t - 1) * n_row + my_row
            mine = [pltpu.make_async_copy(sk_row[0], omega.at[t], sem_s.at[t])]
            away = jnp.bitwise_xor(my_row, help_u[k])
            for o in range(n_row):

                @pl.when(away == o)
                def _(o=o, t=t):
                    pltpu.make_async_copy(sk_row[o], omega.at[t], sem_s.at[t]).start()
            for d in range(n_row):
                j = jnp.bitwise_xor(my_row, d)
                src = raw_u.at[k] if d == 0 else got_u[d - 1].at[t - 1]
                dst = tile.at[t, pl.ds(pl.multiple_of(j * slab, slab), slab)]
                mine.append(pltpu.make_async_copy(src, dst, sem.at[t, d]))
        for c in mine[min(t, 1) :]:
            c.start()
        copies.append(mine)

    row = lax.broadcasted_iota(jnp.int32, (width, width), 0)
    lane = lax.broadcasted_iota(jnp.int32, (width, width), 1)
    eye = (row == lane).astype(jnp.float32)
    sub = lax.broadcasted_iota(jnp.int32, (width, order), 0)
    for t in range(n):
        for c in copies[t]:
            c.wait()
        if t == 0:
            q = rank_l[chunk * n_col + my_col]
        else:
            q = rank_u[chunk * n_col + (t - 1) * n_row + my_row]
        masked = jnp.where(sub < q, omega[t].astype(jnp.float32), 0.0).astype(jnp.bfloat16)
        sketched[t] = mm(masked, tile[t], NT)
        gram = mm(sketched[t], sketched[t], NT, HIGH) + jnp.where(row >= q, eye, 0.0)
        z[t] = jnp.concatenate([gram, eye], axis=1)
    invert_cholesky(z, n, width)
    for t in range(n):
        out = q_l if t == 0 else q_u.at[t - 1]
        basis = mm(z[t, :, width:], sketched[t], NN, HIGH).astype(jnp.bfloat16)
        out[0] = basis
        out[1] = mm(basis, tile[t], NN).astype(jnp.bfloat16)


def factor(chunk, place, help_l, rank_l, help_u, rank_u, tile_l, raw_u, sk_col, sk_row, got_u):
    n_col, n_row = sk_col.shape[0], len(sk_row)
    per = n_col // n_row
    n = 1 + per
    width, order = sk_col.shape[1:]
    smem = pl.BlockSpec(memory_space=pltpu.SMEM)
    hbm = pl.BlockSpec(memory_space=pl.ANY)
    vmem = pl.BlockSpec(memory_space=pltpu.VMEM)
    return pl.pallas_call(
        functools.partial(factor_kernel, n_col, n_row, chunk),
        out_shape=(
            jax.ShapeDtypeStruct((2, width, order), jnp.bfloat16),
            jax.ShapeDtypeStruct((per, 2, width, order), jnp.bfloat16),
        ),
        in_specs=[smem] * 5 + [hbm] * (2 + 2 * n_row),
        out_specs=(vmem, vmem),
        scratch_shapes=[
            pltpu.VMEM((n, width, order), jnp.bfloat16),
            pltpu.VMEM((n, order, order), jnp.bfloat16),
            pltpu.VMEM((n, width, order), jnp.float32),
            pltpu.VMEM((n, width, 2 * width), jnp.float32),
            pltpu.SemaphoreType.DMA((n, n_row)),
            pltpu.SemaphoreType.DMA((n,)),
        ],
        compiler_params=pltpu.CompilerParams(vmem_limit_bytes=56 * 2**20),
        cost_estimate=pl.CostEstimate(flops=35 * 10**9, bytes_accessed=12 * 2**20, transcendentals=0),
        name="factor_tiles",
    )(place, help_l, rank_l, help_u, rank_u, tile_l, raw_u, sk_col, *sk_row, *got_u)


def update_kernel(n_col, n_row, group, *refs):
    place, start, full_l = refs[:3]
    parts = refs[3 : 3 + n_col]
    out, ql, wl, qu, wu, left, sem, sem_t, tr = refs[3 + n_col :]
    my_row = place[0]
    width = ql.shape[1]
    load = pltpu.make_async_copy(start, tr, sem_t)
    load.start()
    for t in range(n_col // n_row):
        for o in range(n_row):
            k = t * n_row + jnp.bitwise_xor(my_row, o)
            src = parts[t * n_row + o]
            pltpu.make_async_copy(src.at[0], qu.at[k], sem.at[2, k]).start()
            pltpu.make_async_copy(src.at[1], wu.at[k], sem.at[3, k]).start()
        for o in range(n_row):
            k = t * n_row + o
            pltpu.make_async_copy(full_l.at[k, 1], wl.at[k], sem.at[1, k]).start()
            pltpu.make_async_copy(full_l.at[k, 0], ql.at[k], sem.at[0, k]).start()
    load.wait()
    out[...] = tr[...].astype(jnp.float32)

    def one_group(g, carry):
        for e in range(group):
            k = g * group + e
            for a, buf in enumerate((ql, wl, qu, wu)):
                pltpu.make_async_copy(buf.at[k], buf.at[k], sem.at[a, k]).wait()
            mid = mm(qu[k], wl[k], NT).astype(jnp.bfloat16)
            left[e * width : (e + 1) * width, :] = mm(mid, ql[k], NN).astype(jnp.bfloat16)
        coeff = wu[pl.ds(g * group, group)].reshape(group * width, wu.shape[2])
        out[...] = out[...] - mm(left[...], coeff, TN)
        return carry

    lax.fori_loop(0, n_col // group, one_group, 0)


def update(place, start, full_l, parts):
    n_col, n_row = full_l.shape[0], len(parts[0])
    width, order = full_l.shape[2:]
    group = 4
    smem = pl.BlockSpec(memory_space=pltpu.SMEM)
    hbm = pl.BlockSpec(memory_space=pl.ANY)
    vmem = pl.BlockSpec(memory_space=pltpu.VMEM)
    held = pltpu.VMEM((n_col, width, order), jnp.bfloat16)
    return pl.pallas_call(
        functools.partial(update_kernel, n_col, n_row, group),
        out_shape=jax.ShapeDtypeStruct(start.shape, jnp.float32),
        in_specs=[smem] + [hbm] * (2 + n_col),
        out_specs=vmem,
        scratch_shapes=[held, held, held, held]
        + [
            pltpu.VMEM((group * width, order), jnp.bfloat16),
            pltpu.SemaphoreType.DMA((4, n_col)),
            pltpu.SemaphoreType.DMA,
            pltpu.VMEM(start.shape, start.dtype),
        ],
        compiler_params=pltpu.CompilerParams(vmem_limit_bytes=56 * 2**20),
        cost_estimate=pl.CostEstimate(flops=15 * 10**9, bytes_accessed=20 * 2**20, transcendentals=0),
        name="update_tile",
    )(place, start, full_l, *parts[0], *parts[1])


def shift(x, axis, size, move):
    return lax.ppermute(x, axis, [(i, move(i)) for i in range(size)])


def exchange_u(raw, n_row):
    me = lax.axis_index("row")
    x = raw.reshape((-1, n_row) + raw.shape[1:])
    return [
        shift(
            lax.dynamic_index_in_dim(x, jnp.bitwise_xor(me, d), 1, False),
            "row",
            n_row,
            lambda i: i ^ d,
        )
        for d in range(1, n_row)
    ]


def spread_row(x, n_row):
    return [x] + [shift(x, "row", n_row, lambda i: i ^ o) for o in range(1, n_row)]


def gather_row_first(pieces, n_row):
    bits = [1 << b for b in range(n_row.bit_length() - 1)]
    out = []
    for number, piece in enumerate(pieces):
        turn = number % len(bits)
        order = bits[turn:] + bits[:turn]
        b = order[0]
        out.append((order[1:], {0: piece, b: shift(piece, "row", n_row, lambda i: i ^ b)}))
    return out


def gather_row_rest(begun, n_row):
    out = []
    for order, held in begun:
        held = dict(held)
        for b in order:
            held.update({o ^ b: shift(p, "row", n_row, lambda i: i ^ b) for o, p in held.items()})
        out.append([held[o] for o in range(n_row)])
    return out


def local(trailing, raw_l, raw_u, sketch, helper_l, helper_u, ranks_l, ranks_u):
    n_col, n_row = lax.axis_size("col"), lax.axis_size("row")
    place = jnp.stack([lax.axis_index("row"), lax.axis_index("col")]).astype(jnp.int32)
    mine_l, mine_u = raw_l[0], raw_u[:, 0]
    chunks = mine_l.shape[0] // n_col
    per = n_col // n_row
    own = jnp.swapaxes(sketch[0, 0], 0, 1)
    sk_col = lax.all_gather(own[None], "col", axis=0, tiled=True)
    sk_row = spread_row(own, n_row)

    def exchange(c, raw):
        part = slice(c * n_col, (c + 1) * n_col)
        tile_l = lax.all_to_all(raw[0][part], "col", 0, 0, tiled=True)
        return tile_l.reshape(-1, tile_l.shape[2]), exchange_u(raw[1][part], n_row)

    def make(c, got):
        return factor(
            c, place, helper_l[0], ranks_l[0], helper_u[:, 0], ranks_u[:, 0],
            got[0], mine_u, sk_col, sk_row, got[1],
        )

    def gather(made, begun):
        full_l = lax.all_gather(made[0][None], "col", axis=0, tiled=True)
        return full_l, gather_row_rest(begun, n_row)

    def begin(made):
        return gather_row_first([made[1][t] for t in range(per)], n_row)

    got = exchange(0, (mine_l, mine_u))
    made = None
    result = trailing
    for c in range(chunks):
        sk_row, later = lax.optimization_barrier((sk_row, (mine_l, mine_u)))
        coming = exchange(c + 1, later) if c + 1 < chunks else None
        if made is not None:
            begun = begin(made)
            held = [h for _, h in begun]
            got, held = lax.optimization_barrier((got, held))
            gathered = gather(made, [(o, h) for (o, _), h in zip(begun, held)])
        fresh = make(c, got)
        if made is not None:
            gathered, fresh = lax.optimization_barrier((gathered, fresh))
            result = update(place, result, *gathered)
        elif coming is not None:
            coming, fresh = lax.optimization_barrier((coming, fresh))
        made, got = fresh, coming
    gathered = gather(made, begin(made))
    return update(place, result, *gathered)


def solution(mesh):
    placed = (
        P("row", "col"),
        P("row", None, "col", None),
        P(None, "col", "row", None),
        P("row", "col", None, None),
        P("row", None),
        P(None, "col"),
        P("row", None),
        P(None, "col"),
    )
    return jax.shard_map(
        local, mesh=mesh, in_specs=placed, out_specs=P("row", "col"), check_vma=False
    )
```

```python
import functools

import jax
import jax.numpy as jnp
from jax import lax
from jax.experimental import pallas as pl
from jax.experimental.pallas import tpu as pltpu
from jax.sharding import PartitionSpec as P

NB = 32
HIGH = lax.Precision.HIGHEST
NN = (((1,), (0,)), ((), ()))
NT = (((1,), (1,)), ((), ()))
TN = (((0,), (0,)), ((), ()))


def mm(a, b, dims, precision=None):
    return lax.dot_general(a, b, dims, precision=precision, preferred_element_type=jnp.float32)


def invert_diagonal(blocks):
    nb = blocks[0].shape[0]
    row = lax.broadcasted_iota(jnp.int32, (nb, 2 * nb), 0)
    lane = lax.broadcasted_iota(jnp.int32, (nb, 2 * nb), 1)
    eye = (lane == row + nb).astype(jnp.float32)
    work = [jnp.concatenate([b, eye[:, nb:]], axis=1) for b in blocks]
    for j in range(nb - 1):
        for n, a in enumerate(work):
            pivot_row = a[j : j + 1, :]
            scaled = pivot_row / a[j : j + 1, j : j + 1]
            work[n] = a - jnp.where(row > j, a[:, j : j + 1], 0.0) * scaled
    out = []
    for a in work:
        d = jnp.sum(jnp.where(lane == row, a, 0.0), axis=1, keepdims=True)
        r = lax.rsqrt(d)
        r = r * (1.5 - 0.5 * d * r * r)
        out.append(a[:, nb:] * r)
    return out


def invert_cholesky(z_ref, n, width):
    for j in range(width // NB):
        lo, hi = j * NB, (j + 1) * NB
        inverses = invert_diagonal([z_ref[t, lo:hi, lo:hi] for t in range(n)])
        for t in range(n):
            panel = mm(inverses[t], z_ref[t, lo:hi, :], NN, HIGH)
            z_ref[t, lo:hi, :] = panel
            if hi < width:
                z_ref[t, hi:, :] = z_ref[t, hi:, :] - mm(panel[:, hi:width], panel, TN, HIGH)


SMEM = pl.BlockSpec(memory_space=pltpu.SMEM)
HBM = pl.BlockSpec(memory_space=pl.ANY)
VMEM = pl.BlockSpec(memory_space=pltpu.VMEM)


def factor_kernel(n_col, n_row, chunk, *refs):
    place, help_l, rank_l, help_u, rank_u = refs[:5]
    tile_l, raw_u, sk_col = refs[5:8]
    sk_row = refs[8 : 8 + n_row]
    got_u = refs[8 + n_row : 7 + 2 * n_row]
    q_l, q_u, omega, tile, sketched, z, sem, sem_s = refs[7 + 2 * n_row :]
    my_row, my_col = place[0], place[1]
    n, width, order = sketched.shape
    slab = order // n_row

    copies = []
    for t in range(n):
        if t == 0:
            k = chunk * n_col + my_col
            mine = [
                pltpu.make_async_copy(sk_row[0], omega.at[t], sem_s.at[t]),
                pltpu.make_async_copy(tile_l, tile.at[t], sem.at[t, 0]),
            ]
            pltpu.make_async_copy(sk_col.at[help_l[k]], omega.at[t], sem_s.at[t]).start()
        else:
            k = chunk * n_col + (t - 1) * n_row + my_row
            mine = [pltpu.make_async_copy(sk_row[0], omega.at[t], sem_s.at[t])]
            away = jnp.bitwise_xor(my_row, help_u[k])
            for o in range(n_row):

                @pl.when(away == o)
                def _(o=o, t=t):
                    pltpu.make_async_copy(sk_row[o], omega.at[t], sem_s.at[t]).start()
            for d in range(n_row):
                j = jnp.bitwise_xor(my_row, d)
                src = raw_u.at[k] if d == 0 else got_u[d - 1].at[t - 1]
                dst = tile.at[t, pl.ds(pl.multiple_of(j * slab, slab), slab)]
                mine.append(pltpu.make_async_copy(src, dst, sem.at[t, d]))
        for c in mine[1:]:
            c.start()
        copies.append(mine)

    row = lax.broadcasted_iota(jnp.int32, (width, width), 0)
    lane = lax.broadcasted_iota(jnp.int32, (width, width), 1)
    eye = (row == lane).astype(jnp.float32)
    sub = lax.broadcasted_iota(jnp.int32, (width, order), 0)
    for t in range(n):
        for c in copies[t]:
            c.wait()
        if t == 0:
            q = rank_l[chunk * n_col + my_col]
        else:
            q = rank_u[chunk * n_col + (t - 1) * n_row + my_row]
        masked = jnp.where(sub < q, omega[t].astype(jnp.float32), 0.0).astype(jnp.bfloat16)
        sketched[t] = mm(masked, tile[t], NT)
        gram = mm(sketched[t], sketched[t], NT, HIGH) + jnp.where(row >= q, eye, 0.0)
        z[t] = jnp.concatenate([gram, eye], axis=1)
    invert_cholesky(z, n, width)
    for t in range(n):
        out = q_l if t == 0 else q_u.at[t - 1]
        basis = mm(z[t, :, width:], sketched[t], NN, HIGH).astype(jnp.bfloat16)
        out[0] = basis
        out[1] = mm(basis, tile[t], NN).astype(jnp.bfloat16)


def factor(chunk, place, help_l, rank_l, help_u, rank_u, tile_l, raw_u, sk_col, sk_row, got_u):
    n_col, n_row = sk_col.shape[0], len(sk_row)
    per = n_col // n_row
    n = 1 + per
    width, order = sk_row[0].shape
    return pl.pallas_call(
        functools.partial(factor_kernel, n_col, n_row, chunk),
        out_shape=(
            jax.ShapeDtypeStruct((2, width, order), jnp.bfloat16),
            jax.ShapeDtypeStruct((per, 2, width, order), jnp.bfloat16),
        ),
        in_specs=[SMEM] * 5 + [HBM] * (2 + 2 * n_row),
        out_specs=(VMEM, VMEM),
        scratch_shapes=[
            pltpu.VMEM((n, width, order), jnp.bfloat16),
            pltpu.VMEM((n, order, order), jnp.bfloat16),
            pltpu.VMEM((n, width, order), jnp.float32),
            pltpu.VMEM((n, width, 2 * width), jnp.float32),
            pltpu.SemaphoreType.DMA((n, n_row)),
            pltpu.SemaphoreType.DMA((n,)),
        ],
        compiler_params=pltpu.CompilerParams(vmem_limit_bytes=56 * 2**20),
        cost_estimate=pl.CostEstimate(flops=35 * 10**11, bytes_accessed=12 * 2**20, transcendentals=0),
        name="factor_tiles",
    )(place, help_l, rank_l, help_u, rank_u, tile_l, raw_u, sk_col, *sk_row, *got_u)


def update_kernel(n_col, n_row, group, *refs):
    place, start, full_l = refs[:3]
    parts = refs[3 : 3 + n_col]
    out, ql, wl, qwu, left, acc, tr, sem, sem_l, sem_t, sem_o = refs[3 + n_col :]
    my_row = place[0]
    width = ql.shape[1]
    rounds = n_col // group
    block = 256
    blocks = start.shape[0] // block

    def load_l(g):
        at = pl.ds(g * group, group)
        return (
            pltpu.make_async_copy(full_l.at[at, 1], wl.at[at], sem_l.at[g, 1]),
            pltpu.make_async_copy(full_l.at[at, 0], ql.at[at], sem_l.at[g, 0]),
        )

    load = pltpu.make_async_copy(start, tr, sem_t)
    for g in range(rounds):
        for c in load_l(g):
            c.start()
        for i in range(g * group, (g + 1) * group):
            t, o = i // n_row, i % n_row
            k = t * n_row + jnp.bitwise_xor(my_row, o)
            pltpu.make_async_copy(parts[i], qwu.at[k], sem.at[k]).start()
    load.start()
    for g in range(rounds):
        for c in load_l(g):
            c.wait()
        for e in range(group):
            k = g * group + e
            pltpu.make_async_copy(parts[0], qwu.at[k], sem.at[k]).wait()
            mid = mm(qwu[k, 0], wl[k], NT).astype(jnp.bfloat16)
            left[e * width : (e + 1) * width, :] = mm(mid, ql[k], NN).astype(jnp.bfloat16)
        coeff = qwu[g * group : (g + 1) * group, 1].reshape(group * width, qwu.shape[3])
        if g == rounds - 1:
            load.wait()
        for b in range(blocks):
            at = slice(b * block, (b + 1) * block)
            part = mm(left[:, at], coeff, TN)
            if g:
                part = acc[at, :] + part
            if g == rounds - 1:
                acc[at, :] = tr[at, :].astype(jnp.float32) - part
                pltpu.make_async_copy(acc.at[at], out.at[at], sem_o.at[b]).start()
            else:
                acc[at, :] = part
    for b in range(blocks):
        at = slice(b * block, (b + 1) * block)
        pltpu.make_async_copy(acc.at[at], out.at[at], sem_o.at[b]).wait()


def update(place, start, full_l, parts):
    n_row = len(parts[0])
    n_col, _, width, order = full_l.shape
    group = 4
    held = pltpu.VMEM((n_col, width, order), jnp.bfloat16)
    return pl.pallas_call(
        functools.partial(update_kernel, n_col, n_row, group),
        out_shape=jax.ShapeDtypeStruct(start.shape, jnp.float32),
        in_specs=[SMEM] + [HBM] * (2 + n_col),
        out_specs=HBM,
        scratch_shapes=[
            held,
            held,
            pltpu.VMEM((n_col, 2, width, order), jnp.bfloat16),
            pltpu.VMEM((group * width, order), jnp.bfloat16),
            pltpu.VMEM(start.shape, jnp.float32),
            pltpu.VMEM(start.shape, start.dtype),
            pltpu.SemaphoreType.DMA((n_col,)),
            pltpu.SemaphoreType.DMA((n_col // group, 2)),
            pltpu.SemaphoreType.DMA,
            pltpu.SemaphoreType.DMA((start.shape[0] // 256,)),
        ],
        compiler_params=pltpu.CompilerParams(vmem_limit_bytes=56 * 2**20),
        cost_estimate=pl.CostEstimate(flops=15 * 10**11, bytes_accessed=20 * 2**20, transcendentals=0),
        name="update_tile",
    )(place, start, full_l, *(p for part in parts for p in part))


def shift(x, axis, size, move):
    return lax.ppermute(x, axis, [(i, move(i)) for i in range(size)])


def outgoing_u(raw, chunk, n_col, n_row):
    me = lax.axis_index("row")
    per = n_col // n_row
    x = raw.reshape((-1, per, n_row) + raw.shape[1:])
    return [
        lax.dynamic_slice(
            x, (chunk, 0, jnp.bitwise_xor(me, d), 0, 0), (1, per, 1) + raw.shape[1:]
        ).reshape((per,) + raw.shape[1:])
        for d in range(1, n_row)
    ]


def exchange_u(sent, n_row):
    return [shift(x, "row", n_row, lambda i: i ^ d) for d, x in enumerate(sent, 1)]


def spread_row(x, n_row):
    return [x] + [shift(x, "row", n_row, lambda i: i ^ o) for o in range(1, n_row)]


def gather_row(pieces, n_row):
    bits = [1 << b for b in range(n_row.bit_length() - 1)]
    out = []
    for number, piece in enumerate(pieces):
        turn = number % len(bits)
        held = {0: piece}
        for b in bits[turn:] + bits[:turn]:
            held.update({o ^ b: shift(p, "row", n_row, lambda i: i ^ b) for o, p in held.items()})
        out.append([held[o] for o in range(n_row)])
    return out


def local(trailing, raw_l, raw_u, sketch, helper_l, helper_u, ranks_l, ranks_u):
    n_col, n_row = lax.axis_size("col"), lax.axis_size("row")
    place = jnp.stack([lax.axis_index("row"), lax.axis_index("col")]).astype(jnp.int32)
    mine_l, mine_u = raw_l[0], raw_u[:, 0]
    chunks = mine_l.shape[0] // n_col
    per = n_col // n_row
    own = jnp.swapaxes(sketch[0, 0], 0, 1)
    sk_col = lax.all_gather(own[None], "col", axis=0, tiled=True)
    sk_row = spread_row(own, n_row)
    result = trailing
    for c in range(chunks):
        tile_l = lax.all_to_all(mine_l[c * n_col : (c + 1) * n_col], "col", 0, 0, tiled=True)
        got_u = exchange_u(outgoing_u(mine_u, c, n_col, n_row), n_row)
        made_l, made_u = factor(
            c, place, helper_l[0], ranks_l[0], helper_u[:, 0], ranks_u[:, 0],
            tile_l.reshape(-1, tile_l.shape[2]), mine_u, sk_col, sk_row, got_u,
        )
        full_l = lax.all_gather(made_l[None], "col", axis=0, tiled=True)
        result = update(place, result, full_l, gather_row([made_u[t] for t in range(per)], n_row))
    return result


def solution(mesh):
    placed = (
        P("row", "col"),
        P("row", None, "col", None),
        P(None, "col", "row", None),
        P("row", "col", None, None),
        P("row", None),
        P(None, "col"),
        P("row", None),
        P(None, "col"),
    )
    return jax.shard_map(
        local, mesh=mesh, in_specs=placed, out_specs=P("row", "col"), check_vma=False
    )
```

```python
import functools

import jax
import jax.numpy as jnp
from jax import lax
from jax.experimental import pallas as pl
from jax.experimental.pallas import tpu as pltpu
from jax.sharding import PartitionSpec as P

NB = 32
PANEL = 8
HIGH = lax.Precision.HIGHEST
NN = (((1,), (0,)), ((), ()))
NT = (((1,), (1,)), ((), ()))
TN = (((0,), (0,)), ((), ()))


def mm(a, b, dims, precision=None):
    return lax.dot_general(a, b, dims, precision=precision, preferred_element_type=jnp.float32)


def invert_diagonal(blocks):
    nb = blocks[0].shape[0]
    row = lax.broadcasted_iota(jnp.int32, (nb, 2 * nb), 0)
    lane = lax.broadcasted_iota(jnp.int32, (nb, 2 * nb), 1)
    eye = (lane == row + nb).astype(jnp.float32)
    work = [jnp.concatenate([b, eye[:, nb:]], axis=1) for b in blocks]
    for p in range(0, nb, PANEL):
        spread = [
            [jnp.broadcast_to(a[:, j : j + 1], a.shape) for j in range(p, p + PANEL)] for a in work
        ]
        for i in range(min(PANEL, nb - 1 - p)):
            j = p + i
            for n, cols in enumerate(spread):
                factors = jnp.where(row > j, cols[i] * (1.0 / cols[i][j : j + 1, :]), 0.0)
                for k in range(i + 1, PANEL):
                    cols[k] = cols[k] - factors * cols[k][j : j + 1, :]
                work[n] = work[n] - factors * work[n][j : j + 1, :]
    out = []
    for a in work:
        d = jnp.sum(jnp.where(lane == row, a, 0.0), axis=1, keepdims=True)
        r = lax.rsqrt(d)
        r = r * (1.5 - 0.5 * d * r * r)
        out.append(a[:, nb:] * r)
    return out


def invert_cholesky(z_ref, n, width):
    for j in range(width // NB):
        lo, hi = j * NB, (j + 1) * NB
        inverses = invert_diagonal([z_ref[t, lo:hi, lo:hi] for t in range(n)])
        for t in range(n):
            panel = mm(inverses[t], z_ref[t, lo:hi, :], NN, HIGH)
            z_ref[t, lo:hi, :] = panel
            if hi < width:
                z_ref[t, hi:, :] = z_ref[t, hi:, :] - mm(panel[:, hi:width], panel, TN, HIGH)


SMEM = pl.BlockSpec(memory_space=pltpu.SMEM)
HBM = pl.BlockSpec(memory_space=pl.ANY)
VMEM = pl.BlockSpec(memory_space=pltpu.VMEM)


def factor_kernel(n_col, n_row, chunk, *refs):
    place, help_l, rank_l, help_u, rank_u = refs[:5]
    tile_l, raw_u, sk_col, own = refs[5:9]
    first_u = refs[9 : 8 + n_row]
    got_u = refs[8 + n_row : 7 + 2 * n_row]
    per = n_col // n_row
    made = refs[7 + 2 * n_row : 8 + 2 * n_row + per]
    omega, tile, sketched, z, sem, sem_s = refs[8 + 2 * n_row + per :]
    my_row, my_col = place[0], place[1]
    n, width, order = sketched.shape
    slab = order // n_row

    copies = []
    for t in range(n):
        if t == 0:
            k = chunk * n_col + my_col
            mine = [
                pltpu.make_async_copy(own, omega.at[t], sem_s.at[t]),
                pltpu.make_async_copy(tile_l, tile.at[t], sem.at[t, 0]),
            ]
            pltpu.make_async_copy(sk_col.at[help_l[k]], omega.at[t], sem_s.at[t]).start()
        else:
            k = chunk * n_col + (t - 1) * n_row + my_row
            mine = [pltpu.make_async_copy(own, omega.at[t], sem_s.at[t])]
            away = jnp.bitwise_xor(my_row, help_u[k])
            for o in range(n_row):

                @pl.when(away == o)
                def _(o=o, t=t):
                    src = first_u[o - 1].at[pl.ds(per * slab, width)] if o else own
                    pltpu.make_async_copy(src, omega.at[t], sem_s.at[t]).start()
            for d in range(n_row):
                j = jnp.bitwise_xor(my_row, d)
                src = raw_u.at[k] if d == 0 else got_u[d - 1].at[pl.ds((t - 1) * slab, slab)]
                dst = tile.at[t, pl.ds(pl.multiple_of(j * slab, slab), slab)]
                mine.append(pltpu.make_async_copy(src, dst, sem.at[t, d]))
        for c in mine[1:]:
            c.start()
        copies.append(mine)

    row = lax.broadcasted_iota(jnp.int32, (width, width), 0)
    lane = lax.broadcasted_iota(jnp.int32, (width, width), 1)
    eye = (row == lane).astype(jnp.float32)
    sub = lax.broadcasted_iota(jnp.int32, (width, order), 0)
    for t in range(n):
        for c in copies[t]:
            c.wait()
        if t == 0:
            q = rank_l[chunk * n_col + my_col]
        else:
            q = rank_u[chunk * n_col + (t - 1) * n_row + my_row]
        masked = jnp.where(sub < q, omega[t].astype(jnp.float32), 0.0).astype(jnp.bfloat16)
        sketched[t] = mm(masked, tile[t], NT)
        gram = mm(sketched[t], sketched[t], NT, HIGH) + jnp.where(row >= q, eye, 0.0)
        z[t] = jnp.concatenate([gram, eye], axis=1)
    invert_cholesky(z, n, width)
    for t in range(n):
        out = made[t]
        basis = mm(z[t, :, width:], sketched[t], NN, HIGH).astype(jnp.bfloat16)
        out[0] = basis
        out[1] = mm(basis, tile[t], NN).astype(jnp.bfloat16)


def factor(chunk, place, help_l, rank_l, help_u, rank_u, tile_l, raw_u, sk_col, own, first_u, got_u):
    n_col, n_row = sk_col.shape[0], len(got_u) + 1
    per = n_col // n_row
    n = 1 + per
    width, order = own.shape
    return pl.pallas_call(
        functools.partial(factor_kernel, n_col, n_row, chunk),
        out_shape=(jax.ShapeDtypeStruct((2, width, order), jnp.bfloat16),) * n,
        in_specs=[SMEM] * 5 + [HBM] * (2 + 2 * n_row),
        out_specs=(VMEM,) * n,
        scratch_shapes=[
            pltpu.VMEM((n, width, order), jnp.bfloat16),
            pltpu.VMEM((n, order, order), jnp.bfloat16),
            pltpu.VMEM((n, width, order), jnp.float32),
            pltpu.VMEM((n, width, 2 * width), jnp.float32),
            pltpu.SemaphoreType.DMA((n, n_row)),
            pltpu.SemaphoreType.DMA((n,)),
        ],
        compiler_params=pltpu.CompilerParams(vmem_limit_bytes=56 * 2**20),
        cost_estimate=pl.CostEstimate(flops=35 * 10**11, bytes_accessed=12 * 2**20, transcendentals=0),
        name="factor_tiles",
    )(place, help_l, rank_l, help_u, rank_u, tile_l, raw_u, sk_col, own, *first_u, *got_u)


def update_kernel(n_col, n_row, group, *refs):
    place, start, full_l = refs[:3]
    parts = refs[3 : 3 + n_col]
    out, ql, wl, qwu, left, acc, tr, sem, sem_l, sem_t, sem_o = refs[3 + n_col :]
    my_row = place[0]
    width = ql.shape[1]
    rounds = n_col // group
    block = 256
    blocks = start.shape[0] // block

    def load_l(g):
        at = pl.ds(g * group, group)
        return (
            pltpu.make_async_copy(full_l.at[at, 1], wl.at[at], sem_l.at[g, 1]),
            pltpu.make_async_copy(full_l.at[at, 0], ql.at[at], sem_l.at[g, 0]),
        )

    load = pltpu.make_async_copy(start, tr, sem_t)
    for g in range(rounds):
        for c in load_l(g):
            c.start()
        for i in range(g * group, (g + 1) * group):
            t, o = i // n_row, i % n_row
            k = t * n_row + jnp.bitwise_xor(my_row, o)
            pltpu.make_async_copy(parts[i], qwu.at[k], sem.at[k]).start()
    load.start()
    for g in range(rounds):
        for c in load_l(g):
            c.wait()
        for e in range(group):
            k = g * group + e
            pltpu.make_async_copy(parts[0], qwu.at[k], sem.at[k]).wait()
            mid = mm(qwu[k, 0], wl[k], NT).astype(jnp.bfloat16)
            left[e * width : (e + 1) * width, :] = mm(mid, ql[k], NN).astype(jnp.bfloat16)
        coeff = qwu[g * group : (g + 1) * group, 1].reshape(group * width, qwu.shape[3])
        if g == rounds - 1:
            load.wait()
        for b in range(blocks):
            at = slice(b * block, (b + 1) * block)
            part = mm(left[:, at], coeff, TN)
            if g:
                part = acc[at, :] + part
            if g == rounds - 1:
                acc[at, :] = tr[at, :].astype(jnp.float32) - part
                pltpu.make_async_copy(acc.at[at], out.at[at], sem_o.at[b]).start()
            else:
                acc[at, :] = part
    for b in range(blocks):
        at = slice(b * block, (b + 1) * block)
        pltpu.make_async_copy(acc.at[at], out.at[at], sem_o.at[b]).wait()


def update(place, start, full_l, parts):
    n_row = len(parts[0])
    n_col, _, width, order = full_l.shape
    group = 4
    held = pltpu.VMEM((n_col, width, order), jnp.bfloat16)
    return pl.pallas_call(
        functools.partial(update_kernel, n_col, n_row, group),
        out_shape=jax.ShapeDtypeStruct(start.shape, jnp.float32),
        in_specs=[SMEM] + [HBM] * (2 + n_col),
        out_specs=HBM,
        scratch_shapes=[
            held,
            held,
            pltpu.VMEM((n_col, 2, width, order), jnp.bfloat16),
            pltpu.VMEM((group * width, order), jnp.bfloat16),
            pltpu.VMEM(start.shape, jnp.float32),
            pltpu.VMEM(start.shape, start.dtype),
            pltpu.SemaphoreType.DMA((n_col,)),
            pltpu.SemaphoreType.DMA((n_col // group, 2)),
            pltpu.SemaphoreType.DMA,
            pltpu.SemaphoreType.DMA((start.shape[0] // 256,)),
        ],
        compiler_params=pltpu.CompilerParams(vmem_limit_bytes=56 * 2**20),
        cost_estimate=pl.CostEstimate(flops=15 * 10**11, bytes_accessed=20 * 2**20, transcendentals=0),
        name="update_tile",
    )(place, start, full_l, *(p for part in parts for p in part))


def shift(x, axis, size, move):
    return lax.ppermute(x, axis, [(i, move(i)) for i in range(size)])


def outgoing_u(raw, chunk, n_col, n_row):
    me = lax.axis_index("row")
    per = n_col // n_row
    x = raw.reshape((-1, per, n_row) + raw.shape[1:])
    return [
        lax.dynamic_slice(
            x, (chunk, 0, jnp.bitwise_xor(me, d), 0, 0), (1, per, 1) + raw.shape[1:]
        ).reshape(-1, raw.shape[2])
        for d in range(1, n_row)
    ]


def exchange_u(sent, n_row):
    return [shift(x, "row", n_row, lambda i: i ^ d) for d, x in enumerate(sent, 1)]


def gather_row(pieces, n_row):
    bits = [1 << b for b in range(n_row.bit_length() - 1)]
    out = []
    for number, piece in enumerate(pieces):
        turn = number % len(bits)
        held = {0: piece}
        for b in bits[turn:] + bits[:turn]:
            held.update({o ^ b: shift(p, "row", n_row, lambda i: i ^ b) for o, p in held.items()})
        out.append([held[o] for o in range(n_row)])
    return out


def local(trailing, raw_l, raw_u, sketch, helper_l, helper_u, ranks_l, ranks_u):
    n_col, n_row = lax.axis_size("col"), lax.axis_size("row")
    place = jnp.stack([lax.axis_index("row"), lax.axis_index("col")]).astype(jnp.int32)
    mine_l, mine_u = raw_l[0], raw_u[:, 0]
    chunks = mine_l.shape[0] // n_col
    own = jnp.swapaxes(sketch[0, 0], 0, 1)
    sk_col = lax.all_gather(own[None], "col", axis=0, tiled=True)
    result, full_l = trailing, None
    for c in range(chunks):
        tile_l = lax.all_to_all(mine_l[c * n_col : (c + 1) * n_col], "col", 0, 0, tiled=True)
        sent_u = outgoing_u(mine_u, c, n_col, n_row)
        if c == 0:
            sent_u = [jnp.concatenate([x, own]) for x in sent_u]
        got_u = exchange_u(sent_u, n_row)
        if c == 0:
            first_u = got_u
        made_l, *made_u = factor(
            c, place, helper_l[0], ranks_l[0], helper_u[:, 0], ranks_u[:, 0],
            tile_l.reshape(-1, tile_l.shape[2]), mine_u, sk_col, own, first_u, got_u,
        )
        if full_l is not None:
            full_l, made_l = lax.optimization_barrier((full_l, made_l))
            result = update(place, result, full_l, full_u)
        full_l = lax.all_gather(made_l[None], "col", axis=0, tiled=True)
        full_u = gather_row(made_u, n_row)
    return update(place, result, full_l, full_u)


def solution(mesh):
    placed = (
        P("row", "col"),
        P("row", None, "col", None),
        P(None, "col", "row", None),
        P("row", "col", None, None),
        P("row", None),
        P(None, "col"),
        P("row", None),
        P(None, "col"),
    )
    return jax.shard_map(
        local, mesh=mesh, in_specs=placed, out_specs=P("row", "col"), check_vma=False
    )
```

```python
import functools

import jax
import jax.numpy as jnp
from jax import lax
from jax.experimental import pallas as pl
from jax.experimental.pallas import tpu as pltpu
from jax.sharding import PartitionSpec as P

NB = 32
PANEL = 8
VMEM_UPDATE = 50
HIGH = lax.Precision.HIGHEST
NN = (((1,), (0,)), ((), ()))
NT = (((1,), (1,)), ((), ()))
TN = (((0,), (0,)), ((), ()))


def mm(a, b, dims, precision=None):
    return lax.dot_general(a, b, dims, precision=precision, preferred_element_type=jnp.float32)


def invert_diagonal(blocks):
    nb = blocks[0].shape[0]
    row = lax.broadcasted_iota(jnp.int32, (nb, 2 * nb), 0)
    lane = lax.broadcasted_iota(jnp.int32, (nb, 2 * nb), 1)
    eye = (lane == row + nb).astype(jnp.float32)
    work = [jnp.concatenate([b, eye[:, nb:]], axis=1) for b in blocks]
    for p in range(0, nb, PANEL):
        spread = [
            [jnp.broadcast_to(a[:, j : j + 1], a.shape) for j in range(p, p + PANEL)] for a in work
        ]
        for i in range(min(PANEL, nb - 1 - p)):
            j = p + i
            for n, cols in enumerate(spread):
                factors = jnp.where(row > j, cols[i] * (1.0 / cols[i][j : j + 1, :]), 0.0)
                for k in range(i + 1, PANEL):
                    cols[k] = cols[k] - factors * cols[k][j : j + 1, :]
                work[n] = work[n] - factors * work[n][j : j + 1, :]
    out = []
    for a in work:
        d = jnp.sum(jnp.where(lane == row, a, 0.0), axis=1, keepdims=True)
        r = lax.rsqrt(d)
        r = r * (1.5 - 0.5 * d * r * r)
        out.append(a[:, nb:] * r)
    return out


def invert_cholesky(z_ref, n, width):
    for j in range(width // NB):
        lo, hi = j * NB, (j + 1) * NB
        inverses = invert_diagonal([z_ref[t, lo:hi, lo:hi] for t in range(n)])
        for t in range(n):
            panel = mm(inverses[t], z_ref[t, lo:hi, :], NN, HIGH)
            z_ref[t, lo:hi, :] = panel
            if hi < width:
                z_ref[t, hi:, :] = z_ref[t, hi:, :] - mm(panel[:, hi:width], panel, TN, HIGH)


SMEM = pl.BlockSpec(memory_space=pltpu.SMEM)
HBM = pl.BlockSpec(memory_space=pl.ANY)
VMEM = pl.BlockSpec(memory_space=pltpu.VMEM)


def factor_kernel(n_col, n_row, chunk, joined, *refs):
    place, help_l, rank_l, help_u, rank_u = refs[:5]
    tile_l, raw_u, sk_col, own = refs[5:9]
    first_u = refs[9 : 8 + n_row]
    got_u = refs[8 + n_row : 7 + 2 * n_row]
    per = n_col // n_row
    outs = 2 if joined else 1 + per
    made = refs[7 + 2 * n_row : 7 + 2 * n_row + outs]
    omega, tile, sketched, z, sem, sem_s = refs[7 + 2 * n_row + outs :]
    my_row, my_col = place[0], place[1]
    n, width, order = sketched.shape
    slab = order // n_row

    copies = []
    for t in range(n):
        if t == 0:
            k = chunk * n_col + my_col
            mine = [
                pltpu.make_async_copy(own, omega.at[t], sem_s.at[t]),
                pltpu.make_async_copy(tile_l, tile.at[t], sem.at[t, 0]),
            ]
            pltpu.make_async_copy(sk_col.at[help_l[k]], omega.at[t], sem_s.at[t]).start()
        else:
            k = chunk * n_col + (t - 1) * n_row + my_row
            mine = [pltpu.make_async_copy(own, omega.at[t], sem_s.at[t])]
            away = jnp.bitwise_xor(my_row, help_u[k])
            for o in range(n_row):

                @pl.when(away == o)
                def _(o=o, t=t):
                    src = first_u[o - 1].at[pl.ds(per * slab, width)] if o else own
                    pltpu.make_async_copy(src, omega.at[t], sem_s.at[t]).start()
            for d in range(n_row):
                j = jnp.bitwise_xor(my_row, d)
                src = raw_u.at[k] if d == 0 else got_u[d - 1].at[pl.ds((t - 1) * slab, slab)]
                dst = tile.at[t, pl.ds(pl.multiple_of(j * slab, slab), slab)]
                mine.append(pltpu.make_async_copy(src, dst, sem.at[t, d]))
        for c in mine[1:]:
            c.start()
        copies.append(mine)

    row = lax.broadcasted_iota(jnp.int32, (width, width), 0)
    lane = lax.broadcasted_iota(jnp.int32, (width, width), 1)
    eye = (row == lane).astype(jnp.float32)
    sub = lax.broadcasted_iota(jnp.int32, (width, order), 0)
    for t in range(n):
        for c in copies[t]:
            c.wait()
        if t == 0:
            q = rank_l[chunk * n_col + my_col]
        else:
            q = rank_u[chunk * n_col + (t - 1) * n_row + my_row]
        masked = jnp.where(sub < q, omega[t].astype(jnp.float32), 0.0).astype(jnp.bfloat16)
        sketched[t] = mm(masked, tile[t], NT)
        gram = mm(sketched[t], sketched[t], NT, HIGH) + jnp.where(row >= q, eye, 0.0)
        z[t] = jnp.concatenate([gram, eye], axis=1)
    invert_cholesky(z, n, width)
    for t in range(n):
        out = made[1].at[t - 1] if joined and t else made[t]
        basis = mm(z[t, :, width:], sketched[t], NN, HIGH).astype(jnp.bfloat16)
        out[0] = basis
        out[1] = mm(basis, tile[t], NN).astype(jnp.bfloat16)


def factor(chunk, place, help_l, rank_l, help_u, rank_u, tile_l, raw_u, sk_col, own, first_u, got_u, joined):
    n_col, n_row = sk_col.shape[0], len(got_u) + 1
    per = n_col // n_row
    n = 1 + per
    width, order = own.shape
    one = jax.ShapeDtypeStruct((2, width, order), jnp.bfloat16)
    both = jax.ShapeDtypeStruct((per, 2, width, order), jnp.bfloat16)
    made = (one, both) if joined else (one,) * n
    return pl.pallas_call(
        functools.partial(factor_kernel, n_col, n_row, chunk, joined),
        out_shape=made,
        in_specs=[SMEM] * 5 + [HBM] * (2 + 2 * n_row),
        out_specs=(VMEM,) * len(made),
        scratch_shapes=[
            pltpu.VMEM((n, width, order), jnp.bfloat16),
            pltpu.VMEM((n, order, order), jnp.bfloat16),
            pltpu.VMEM((n, width, order), jnp.float32),
            pltpu.VMEM((n, width, 2 * width), jnp.float32),
            pltpu.SemaphoreType.DMA((n, n_row)),
            pltpu.SemaphoreType.DMA((n,)),
        ],
        compiler_params=pltpu.CompilerParams(vmem_limit_bytes=56 * 2**20),
        cost_estimate=pl.CostEstimate(flops=35 * 10**11, bytes_accessed=12 * 2**20, transcendentals=0),
        name="factor_tiles",
    )(place, help_l, rank_l, help_u, rank_u, tile_l, raw_u, sk_col, own, *first_u, *got_u)


def update_kernel(n_col, n_row, *refs):
    place, start, full_l = refs[:3]
    out, ql, wl, left, acc, sem_l, sem_o = refs[-7:]
    parts = refs[3:-7]
    if len(parts) == n_row:
        parts = [p.at[t] for t in range(n_col // n_row) for p in parts]
    my_row = place[0]
    width = ql.shape[1]
    rounds = n_col // n_row
    block = 256
    blocks = start.shape[0] // block

    def load_l(g):
        at = pl.ds(g * n_row, n_row)
        return (
            pltpu.make_async_copy(full_l.at[at, 1], wl.at[at], sem_l.at[g, 1]),
            pltpu.make_async_copy(full_l.at[at, 0], ql.at[at], sem_l.at[g, 0]),
        )

    for g in range(rounds):
        for c in load_l(g):
            c.start()
    for g in range(rounds):
        mine = parts[g * n_row : (g + 1) * n_row]
        load_w, load_q = load_l(g)
        load_w.wait()
        mids = []
        for o, part in enumerate(mine):
            k = g * n_row + jnp.bitwise_xor(my_row, o)
            mids.append(mm(part[0], wl[k], NT).astype(jnp.bfloat16))
        load_q.wait()
        for o, mid in enumerate(mids):
            k = g * n_row + jnp.bitwise_xor(my_row, o)
            left[o * width : (o + 1) * width, :] = mm(mid, ql[k], NN).astype(jnp.bfloat16)
        coeff = jnp.concatenate([part[1] for part in mine], axis=0)
        for b in range(blocks):
            at = slice(b * block, (b + 1) * block)
            done = mm(left[:, at], coeff, TN)
            if g:
                done = acc[at, :] + done
            if g == rounds - 1:
                acc[at, :] = start[at, :].astype(jnp.float32) - done
                pltpu.make_async_copy(acc.at[at], out.at[at], sem_o.at[b]).start()
            else:
                acc[at, :] = done
    for b in range(blocks):
        at = slice(b * block, (b + 1) * block)
        pltpu.make_async_copy(acc.at[at], out.at[at], sem_o.at[b]).wait()


def update(place, start, full_l, parts):
    n_row = lax.axis_size("row")
    n_col, _, width, order = full_l.shape
    held = pltpu.VMEM((n_col, width, order), jnp.bfloat16)
    return pl.pallas_call(
        functools.partial(update_kernel, n_col, n_row),
        out_shape=jax.ShapeDtypeStruct(start.shape, jnp.float32),
        in_specs=[SMEM, VMEM, HBM] + [VMEM] * len(parts),
        out_specs=HBM,
        scratch_shapes=[
            held,
            held,
            pltpu.VMEM((n_row * width, order), jnp.bfloat16),
            pltpu.VMEM(start.shape, jnp.float32),
            pltpu.SemaphoreType.DMA((n_col // n_row, 2)),
            pltpu.SemaphoreType.DMA((start.shape[0] // 256,)),
        ],
        compiler_params=pltpu.CompilerParams(vmem_limit_bytes=VMEM_UPDATE * 2**20),
        cost_estimate=pl.CostEstimate(flops=15 * 10**11, bytes_accessed=20 * 2**20, transcendentals=0),
        name="update_tile",
    )(place, start, full_l, *parts)


def shift(x, axis, size, move):
    return lax.ppermute(x, axis, [(i, move(i)) for i in range(size)])


def outgoing_u(raw, chunk, n_col, n_row):
    me = lax.axis_index("row")
    per = n_col // n_row
    x = raw.reshape((-1, per, n_row) + raw.shape[1:])
    return [
        lax.dynamic_slice(
            x, (chunk, 0, jnp.bitwise_xor(me, d), 0, 0), (1, per, 1) + raw.shape[1:]
        ).reshape(-1, raw.shape[2])
        for d in range(1, n_row)
    ]


def exchange_u(sent, n_row):
    return [shift(x, "row", n_row, lambda i: i ^ d) for d, x in enumerate(sent, 1)]


def spread_row(x, n_row):
    return [x] + [shift(x, "row", n_row, lambda i: i ^ o) for o in range(1, n_row)]


def gather_row(pieces, n_row):
    bits = [1 << b for b in range(n_row.bit_length() - 1)]
    out = []
    for number, piece in enumerate(pieces):
        turn = number % len(bits)
        held = {0: piece}
        for b in bits[turn:] + bits[:turn]:
            held.update({o ^ b: shift(p, "row", n_row, lambda i: i ^ b) for o, p in held.items()})
        out += [held[o] for o in range(n_row)]
    return out


def local(trailing, raw_l, raw_u, sketch, helper_l, helper_u, ranks_l, ranks_u):
    n_col, n_row = lax.axis_size("col"), lax.axis_size("row")
    place = jnp.stack([lax.axis_index("row"), lax.axis_index("col")]).astype(jnp.int32)
    mine_l, mine_u = raw_l[0], raw_u[:, 0]
    chunks = mine_l.shape[0] // n_col
    own = jnp.swapaxes(sketch[0, 0], 0, 1)
    sk_col = lax.all_gather(own[None], "col", axis=0, tiled=True)
    result, full_l = trailing, None
    for c in range(chunks):
        if c == 1:
            mine_l, first_u[0] = lax.optimization_barrier((mine_l, first_u[0]))
        tile_l = lax.all_to_all(mine_l[c * n_col : (c + 1) * n_col], "col", 0, 0, tiled=True)
        sent_u = outgoing_u(mine_u, c, n_col, n_row)
        if c == 0:
            sent_u = [jnp.concatenate([x, own]) for x in sent_u]
        got_u = exchange_u(sent_u, n_row)
        if c == 0:
            first_u = got_u
        made_l, *made_u = factor(
            c, place, helper_l[0], ranks_l[0], helper_u[:, 0], ranks_u[:, 0],
            tile_l.reshape(-1, tile_l.shape[2]), mine_u, sk_col, own, first_u, got_u,
            c + 1 < chunks,
        )
        if full_l is not None:
            full_l, made_l = lax.optimization_barrier((full_l, made_l))
            result = update(place, result, full_l, full_u)
        full_l = lax.all_gather(made_l[None], "col", axis=0, tiled=True)
        last = c + 1 == chunks
        full_u = gather_row(made_u, n_row) if last else spread_row(made_u[0], n_row)
    return update(place, result, full_l, full_u)


def solution(mesh):
    placed = (
        P("row", "col"),
        P("row", None, "col", None),
        P(None, "col", "row", None),
        P("row", "col", None, None),
        P("row", None),
        P(None, "col"),
        P("row", None),
        P(None, "col"),
    )
    return jax.shard_map(
        local, mesh=mesh, in_specs=placed, out_specs=P("row", "col"), check_vma=False
    )
```

```python
import functools

import jax
import jax.numpy as jnp
from jax import lax
from jax.experimental import pallas as pl
from jax.experimental.pallas import tpu as pltpu
from jax.sharding import PartitionSpec as P

NB = 64
PANEL = 8
VMEM_UPDATE = 56
HIGH = lax.Precision.HIGHEST
NN = (((1,), (0,)), ((), ()))
NT = (((1,), (1,)), ((), ()))
TN = (((0,), (0,)), ((), ()))


def mm(a, b, dims, precision=None):
    return lax.dot_general(a, b, dims, precision=precision, preferred_element_type=jnp.float32)


def invert_diagonal(blocks):
    nb = blocks[0].shape[0]
    row = lax.broadcasted_iota(jnp.int32, (nb, 2 * nb), 0)
    lane = lax.broadcasted_iota(jnp.int32, (nb, 2 * nb), 1)
    eye = (lane == row + nb).astype(jnp.float32)
    work = [jnp.concatenate([b, eye[:, nb:]], axis=1) for b in blocks]
    for p in range(0, nb, PANEL):
        spread = [
            [jnp.broadcast_to(a[:, j : j + 1], a.shape) for j in range(p, p + PANEL)] for a in work
        ]
        for i in range(min(PANEL, nb - 1 - p)):
            j = p + i
            for n, cols in enumerate(spread):
                factors = jnp.where(row > j, cols[i] * (1.0 / cols[i][j : j + 1, :]), 0.0)
                for k in range(i + 1, PANEL):
                    cols[k] = cols[k] - factors * cols[k][j : j + 1, :]
                work[n] = work[n] - factors * work[n][j : j + 1, :]
    out = []
    for a in work:
        d = jnp.sum(jnp.where(lane == row, a, 0.0), axis=1, keepdims=True)
        r = lax.rsqrt(d)
        r = r * (1.5 - 0.5 * d * r * r)
        out.append(a[:, nb:] * r)
    return out


def invert_cholesky(z_ref, n, width):
    for j in range(width // NB):
        lo, hi = j * NB, (j + 1) * NB
        inverses = invert_diagonal([z_ref[t, lo:hi, lo:hi] for t in range(n)])
        for t in range(n):
            panel = mm(inverses[t], z_ref[t, lo:hi, :], NN, HIGH)
            z_ref[t, lo:hi, :] = panel
            if hi < width:
                z_ref[t, hi:, :] = z_ref[t, hi:, :] - mm(panel[:, hi:width], panel, TN, HIGH)


SMEM = pl.BlockSpec(memory_space=pltpu.SMEM)
HBM = pl.BlockSpec(memory_space=pl.ANY)
VMEM = pl.BlockSpec(memory_space=pltpu.VMEM)


def factor_kernel(n_col, n_row, chunk, joined, *refs):
    place, help_l, rank_l, help_u, rank_u = refs[:5]
    tile_l, raw_u, sk_col, own = refs[5:9]
    first_u = refs[9 : 8 + n_row]
    got_u = refs[8 + n_row : 7 + 2 * n_row]
    per = n_col // n_row
    outs = 2 if joined else 1 + per
    made = refs[7 + 2 * n_row : 7 + 2 * n_row + outs]
    omega, tile, sketched, z, sem, sem_s = refs[7 + 2 * n_row + outs :]
    my_row, my_col = place[0], place[1]
    n, width, order = sketched.shape
    slab = order // n_row

    copies = []
    for t in range(n):
        if t == 0:
            k = chunk * n_col + my_col
            mine = [
                pltpu.make_async_copy(own, omega.at[t], sem_s.at[t]),
                pltpu.make_async_copy(tile_l, tile.at[t], sem.at[t, 0]),
            ]
            pltpu.make_async_copy(sk_col.at[help_l[k]], omega.at[t], sem_s.at[t]).start()
        else:
            k = chunk * n_col + (t - 1) * n_row + my_row
            mine = [pltpu.make_async_copy(own, omega.at[t], sem_s.at[t])]
            away = jnp.bitwise_xor(my_row, help_u[k])
            for o in range(n_row):

                @pl.when(away == o)
                def _(o=o, t=t):
                    src = first_u[o - 1].at[pl.ds(per * slab, width)] if o else own
                    pltpu.make_async_copy(src, omega.at[t], sem_s.at[t]).start()
            for d in range(n_row):
                j = jnp.bitwise_xor(my_row, d)
                src = raw_u.at[k] if d == 0 else got_u[d - 1].at[pl.ds((t - 1) * slab, slab)]
                dst = tile.at[t, pl.ds(pl.multiple_of(j * slab, slab), slab)]
                mine.append(pltpu.make_async_copy(src, dst, sem.at[t, d]))
        for c in mine[1:]:
            c.start()
        copies.append(mine)

    row = lax.broadcasted_iota(jnp.int32, (width, width), 0)
    lane = lax.broadcasted_iota(jnp.int32, (width, width), 1)
    eye = (row == lane).astype(jnp.float32)
    sub = lax.broadcasted_iota(jnp.int32, (width, order), 0)
    for t in range(n):
        for c in copies[t]:
            c.wait()
        if t == 0:
            q = rank_l[chunk * n_col + my_col]
        else:
            q = rank_u[chunk * n_col + (t - 1) * n_row + my_row]
        masked = jnp.where(sub < q, omega[t].astype(jnp.float32), 0.0).astype(jnp.bfloat16)
        sketched[t] = mm(masked, tile[t], NT)
        gram = mm(sketched[t], sketched[t], NT, HIGH) + jnp.where(row >= q, eye, 0.0)
        z[t] = jnp.concatenate([gram, eye], axis=1)
    invert_cholesky(z, n, width)
    for t in range(n):
        out = made[1].at[t - 1] if joined and t else made[t]
        basis = mm(z[t, :, width:], sketched[t], NN, HIGH).astype(jnp.bfloat16)
        out[0] = basis
        out[1] = mm(basis, tile[t], NN).astype(jnp.bfloat16)


def factor(chunk, place, help_l, rank_l, help_u, rank_u, tile_l, raw_u, sk_col, own, first_u, got_u, joined):
    n_col, n_row = sk_col.shape[0], len(got_u) + 1
    per = n_col // n_row
    n = 1 + per
    width, order = own.shape
    one = jax.ShapeDtypeStruct((2, width, order), jnp.bfloat16)
    both = jax.ShapeDtypeStruct((per, 2, width, order), jnp.bfloat16)
    made = (one, both) if joined else (one,) * n
    return pl.pallas_call(
        functools.partial(factor_kernel, n_col, n_row, chunk, joined),
        out_shape=made,
        in_specs=[SMEM] * 5 + [HBM] * (2 + 2 * n_row),
        out_specs=(VMEM,) * len(made),
        scratch_shapes=[
            pltpu.VMEM((n, width, order), jnp.bfloat16),
            pltpu.VMEM((n, order, order), jnp.bfloat16),
            pltpu.VMEM((n, width, order), jnp.float32),
            pltpu.VMEM((n, width, 2 * width), jnp.float32),
            pltpu.SemaphoreType.DMA((n, n_row)),
            pltpu.SemaphoreType.DMA((n,)),
        ],
        compiler_params=pltpu.CompilerParams(vmem_limit_bytes=56 * 2**20),
        cost_estimate=pl.CostEstimate(flops=35 * 10**11, bytes_accessed=12 * 2**20, transcendentals=0),
        name="factor_tiles",
    )(place, help_l, rank_l, help_u, rank_u, tile_l, raw_u, sk_col, own, *first_u, *got_u)


def update_kernel(n_col, n_row, *refs):
    place, start, full_l = refs[:3]
    out, ql, wl, qwu, left, acc, tr, sem_l, sem_u, sem_t, sem_o = refs[-11:]
    parts = refs[3:-11]
    if len(parts) == n_row:
        parts = [p.at[t] for t in range(n_col // n_row) for p in parts]
    my_row = place[0]
    width = ql.shape[1]
    rounds = n_col // n_row
    block = 256
    blocks = start.shape[0] // block

    def load_l(g):
        at = pl.ds(g * n_row, n_row)
        return (
            pltpu.make_async_copy(full_l.at[at, 1], wl.at[at], sem_l.at[g, 1]),
            pltpu.make_async_copy(full_l.at[at, 0], ql.at[at], sem_l.at[g, 0]),
        )

    def load_u(i):
        return pltpu.make_async_copy(parts[i], qwu.at[i], sem_u.at[i])

    def load(g):
        load_w, load_q = load_l(g)
        load_w.start()
        for i in range(g * n_row, (g + 1) * n_row):
            load_u(i).start()
        load_q.start()

    load_start = pltpu.make_async_copy(start, tr, sem_t)
    load(0)
    for g in range(rounds):
        mine = [qwu.at[i] for i in range(g * n_row, (g + 1) * n_row)]
        load_w, load_q = load_l(g)
        load_w.wait()
        mids = []
        for o, part in enumerate(mine):
            load_u(g * n_row + o).wait()
            k = g * n_row + jnp.bitwise_xor(my_row, o)
            mids.append(mm(part[0], wl[k], NT).astype(jnp.bfloat16))
        load_q.wait()
        if g + 1 < rounds:
            load(g + 1)
        if g == 0:
            load_start.start()
        if g == rounds - 1:
            load_start.wait()
        for o, mid in enumerate(mids):
            k = g * n_row + jnp.bitwise_xor(my_row, o)
            left[o * width : (o + 1) * width, :] = mm(mid, ql[k], NN).astype(jnp.bfloat16)
        coeff = jnp.concatenate([part[1] for part in mine], axis=0)
        for b in range(blocks):
            at = slice(b * block, (b + 1) * block)
            done = mm(left[:, at], coeff, TN)
            if g:
                done = acc[at, :] + done
            if g == rounds - 1:
                acc[at, :] = tr[at, :].astype(jnp.float32) - done
                pltpu.make_async_copy(acc.at[at], out.at[at], sem_o.at[b]).start()
            else:
                acc[at, :] = done
    for b in range(blocks):
        at = slice(b * block, (b + 1) * block)
        pltpu.make_async_copy(acc.at[at], out.at[at], sem_o.at[b]).wait()


def update(place, start, full_l, parts):
    n_row = lax.axis_size("row")
    n_col, _, width, order = full_l.shape
    held = pltpu.VMEM((n_col, width, order), jnp.bfloat16)
    return pl.pallas_call(
        functools.partial(update_kernel, n_col, n_row),
        out_shape=jax.ShapeDtypeStruct(start.shape, jnp.float32),
        in_specs=[SMEM, HBM, HBM] + [HBM] * len(parts),
        out_specs=HBM,
        scratch_shapes=[
            held,
            held,
            pltpu.VMEM((n_col, 2, width, order), jnp.bfloat16),
            pltpu.VMEM((n_row * width, order), jnp.bfloat16),
            pltpu.VMEM(start.shape, jnp.float32),
            pltpu.VMEM(start.shape, start.dtype),
            pltpu.SemaphoreType.DMA((n_col // n_row, 2)),
            pltpu.SemaphoreType.DMA((n_col,)),
            pltpu.SemaphoreType.DMA,
            pltpu.SemaphoreType.DMA((start.shape[0] // 256,)),
        ],
        compiler_params=pltpu.CompilerParams(vmem_limit_bytes=VMEM_UPDATE * 2**20),
        cost_estimate=pl.CostEstimate(flops=15 * 10**11, bytes_accessed=20 * 2**20, transcendentals=0),
        name="update_tile",
    )(place, start, full_l, *parts)


def shift(x, axis, size, move):
    return lax.ppermute(x, axis, [(i, move(i)) for i in range(size)])


def outgoing_u(raw, chunk, n_col, n_row):
    me = lax.axis_index("row")
    per = n_col // n_row
    x = raw.reshape((-1, per, n_row) + raw.shape[1:])
    return [
        lax.dynamic_slice(
            x, (chunk, 0, jnp.bitwise_xor(me, d), 0, 0), (1, per, 1) + raw.shape[1:]
        ).reshape(-1, raw.shape[2])
        for d in range(1, n_row)
    ]


def exchange_u(sent, n_row):
    return [shift(x, "row", n_row, lambda i: i ^ d) for d, x in enumerate(sent, 1)]


def spread_row(x, n_row):
    return [x] + [shift(x, "row", n_row, lambda i: i ^ o) for o in range(1, n_row)]


def gather_row(pieces, n_row):
    bits = [1 << b for b in range(n_row.bit_length() - 1)]
    out = []
    for number, piece in enumerate(pieces):
        turn = number % len(bits)
        held = {0: piece}
        for b in bits[turn:] + bits[:turn]:
            held.update({o ^ b: shift(p, "row", n_row, lambda i: i ^ b) for o, p in held.items()})
        out += [held[o] for o in range(n_row)]
    return out


def local(trailing, raw_l, raw_u, sketch, helper_l, helper_u, ranks_l, ranks_u):
    n_col, n_row = lax.axis_size("col"), lax.axis_size("row")
    place = jnp.stack([lax.axis_index("row"), lax.axis_index("col")]).astype(jnp.int32)
    mine_l, mine_u = raw_l[0], raw_u[:, 0]
    chunks = mine_l.shape[0] // n_col
    own = jnp.swapaxes(sketch[0, 0], 0, 1)
    sk_col = lax.all_gather(own[None], "col", axis=0, tiled=True)
    result, full_l = trailing, None
    for c in range(chunks):
        if c == 1:
            mine_l, first_u[0] = lax.optimization_barrier((mine_l, first_u[0]))
        tile_l = lax.all_to_all(mine_l[c * n_col : (c + 1) * n_col], "col", 0, 0, tiled=True)
        sent_u = outgoing_u(mine_u, c, n_col, n_row)
        if c == 0:
            sent_u = [jnp.concatenate([x, own]) for x in sent_u]
        got_u = exchange_u(sent_u, n_row)
        if c == 0:
            first_u = got_u
        made_l, *made_u = factor(
            c, place, helper_l[0], ranks_l[0], helper_u[:, 0], ranks_u[:, 0],
            tile_l.reshape(-1, tile_l.shape[2]), mine_u, sk_col, own, first_u, got_u,
            c + 1 < chunks,
        )
        if full_l is not None:
            full_l, made_l = lax.optimization_barrier((full_l, made_l))
            result = update(place, result, full_l, full_u)
        full_l = lax.all_gather(made_l[None], "col", axis=0, tiled=True)
        last = c + 1 == chunks
        full_u = gather_row(made_u, n_row) if last else spread_row(made_u[0], n_row)
    return update(place, result, full_l, full_u)


def solution(mesh):
    placed = (
        P("row", "col"),
        P("row", None, "col", None),
        P(None, "col", "row", None),
        P("row", "col", None, None),
        P("row", None),
        P(None, "col"),
        P("row", None),
        P(None, "col"),
    )
    return jax.shard_map(
        local, mesh=mesh, in_specs=placed, out_specs=P("row", "col"), check_vma=False
    )
```
